256 devices in a mesh: row: 16 (over z, core), col: 16 (over y, x).
Axes of the slice: x: 4, y: 4, z: 8, core: 2. Of those that a mesh axis runs over, the one named last changes fastest.
Arguments:
- src_emb: float32 [32, 262144], P(None, ('row', 'col')), may hold values from -6 to 6
- tgt_emb: float32 [32, 32768], P(None, 'col'), may hold values from -6 to 6
- log_a: float32 [262144], P(('row', 'col')), may hold values from -5 to 5
- log_b: float32 [32768], P('col'), may hold values from -5 to 5
- g_init: float32 [32768], P('col'), may hold values from -15 to 425
- lists: int32 [1024, 16, 4], P('row', 'col'), may hold values from 0 to 7, as said below
- counts: int32 [1024, 16], P('row', 'col'), may hold values from 1 to 4, as said below
Outputs:
- f_pot: float32 [262144], P(('row', 'col'))
- g_pot: float32 [32768], P('col')
The draws below stay inside these ranges and needn't reach their ends.
Inputs may be any that keep to these rules, and one draw needn't show every extreme that they name: `lists`: within one list the slots hold different blocks, and slot 0 of source block b holds b mod 8. `counts`: source block 0 has all 4 slots valid in every index of col.
All inputs are finite; a program needn't handle non-finite values.
Results may differ from the reference program's by a relative error of at most 0.000067.
Values sent between devices are 32-bit elements; how exact they have to be, the bound alone decides.
A program may use at most 64 MiB of HBM per device.

```python
import jax
import jax.numpy as jnp
from jax import lax

LAT = 32
BLOCK_CELLS = 256
TBC = 8
KC = 4
SB = 1024
TB = 128
NS = 262144
NT = 32768
N_COL = 16


def draw_g_init(key, part):
    key = jax.random.fold_in(key, 3)
    first = jax.random.fold_in(key, 0)
    return jnp.clip(3.0 * jax.random.normal(first, (NT,)), -15.0, 15.0).astype(jnp.float32)


def draw_lists(key, part):
    key = jax.random.fold_in(key, 5)
    scores = jax.random.randint(key, (SB, N_COL, TBC - 1), 0, 2 ** 20) * TBC
    scores = scores + jnp.arange(TBC - 1, dtype=jnp.int32)[None, None, :]
    order = jnp.argsort(scores, axis=-1, stable=True).astype(jnp.int32) + 1
    steps = jnp.concatenate([jnp.zeros((SB, N_COL, 1), jnp.int32), order[:, :, :KC - 1]], axis=-1)
    rows = jnp.arange(SB, dtype=jnp.int32)[:, None, None]
    return ((rows + steps) % TBC).astype(jnp.int32)


def draw_counts(key, part):
    key = jax.random.fold_in(key, 7)
    drawn = jax.random.randint(key, (SB, N_COL), 1, KC + 1)
    rows = jnp.arange(SB, dtype=jnp.int32)[:, None]
    return jnp.where(rows == 0, KC, drawn).astype(jnp.int32)


def shard_levels(own_key, dims, cuts, low, top_value):
    gain = 1.0
    for position, parts in cuts:
        draws = jax.random.uniform(jax.random.fold_in(jax.random.fold_in(own_key, 6), position), (parts,), jnp.float32, low / len(cuts), top_value / len(cuts))
        gain = gain * jnp.repeat(jnp.exp(draws), dims[position] // parts).reshape((-1,) + (1,) * (len(dims) - 1 - position))
    return gain


def normal_values(key, extent, scale, bound, shards=(), kind=jnp.bfloat16):
    values = jax.random.normal(key, extent, jnp.float32) * scale
    if len(shards) > 0:
        values = shard_levels(key, extent, shards, -0.22, 0.18) * values
    return jnp.clip(values, min=-bound, max=bound).astype(kind)


def setup_inputs(seed: int = 0) -> dict:
    key_list = jax.random.split(jax.random.key(seed), 8)
    return {
        "src_emb": normal_values(key_list[0], (LAT, NS), 1.0, 6.0, ((1, 256),), jnp.float32),
        "tgt_emb": normal_values(key_list[1], (LAT, NT), 1.0, 6.0, ((1, 16),), jnp.float32),
        "log_a": normal_values(key_list[2], (NS,), 1.0, 5.0, ((0, 256),), jnp.float32),
        "log_b": normal_values(key_list[3], (NT,), 1.0, 5.0, ((0, 16),), jnp.float32),
        "g_init": draw_g_init(jax.random.fold_in(key_list[7], 71), 0),
        "lists": draw_lists(jax.random.fold_in(key_list[7], 71), 0),
        "counts": draw_counts(jax.random.fold_in(key_list[7], 71), 0),
    }


EPSILON = 2.0
NEG = -1.0e30


def pair_cost(xb, yb):
    cross = jnp.einsum('li,elj->eij', xb, yb, precision=lax.Precision.HIGHEST)
    xx = jnp.sum(xb * xb, axis=0)
    yy = jnp.sum(yb * yb, axis=1)
    return 0.5 * (xx[None, :, None] + yy[:, None, :]) - cross


def reference(src_emb, tgt_emb, log_a, log_b, g_init, lists, counts):
    cross_blocks = src_emb.reshape(LAT, SB, BLOCK_CELLS).transpose(1, 0, 2)
    yblocks = tgt_emb.reshape(LAT, TB, BLOCK_CELLS).transpose(1, 0, 2)
    gblocks = g_init.reshape(TB, BLOCK_CELLS)
    owner = (jnp.arange(N_COL, dtype=jnp.int32) * TBC).astype(jnp.int32)
    glob = (lists + owner[None, :, None]).reshape(SB, N_COL * KC).astype(jnp.int32)
    valid = (jnp.arange(KC, dtype=jnp.int32)[None, None, :] < counts[:, :, None]).reshape(SB, N_COL * KC)

    def row_stats(args):
        xb, cell_index, okay = args
        cost = pair_cost(xb, yblocks[cell_index])
        score = (gblocks[cell_index][:, None, :] - cost) / EPSILON
        score = jnp.where(okay[:, None, None], score, NEG)
        top = jnp.max(score, axis=(0, 2))
        total = jnp.sum(jnp.exp(score - top[None, :, None]), axis=(0, 2))
        return top, total

    top, total = lax.map(row_stats, (cross_blocks, glob, valid))
    f_pot = EPSILON * log_a - EPSILON * (top + jnp.log(total)).reshape(NS)

    fblocks = f_pot.reshape(SB, BLOCK_CELLS)

    def col_stats(args):
        xb, fb, cell_index = args
        cost = pair_cost(xb, yblocks[cell_index])
        score = (fb[None, :, None] - cost) / EPSILON
        peak_value = jnp.max(score, axis=1)
        mass_weights = jnp.sum(jnp.exp(score - peak_value[:, None, :]), axis=1)
        return peak_value, mass_weights

    peak_value, mass_weights = lax.map(col_stats, (cross_blocks, fblocks, glob))
    seg = jnp.where(valid, glob, TB).reshape(-1).astype(jnp.int32)
    flat_valid = valid.reshape(-1)
    peak_value = jnp.where(flat_valid[:, None], peak_value.reshape(-1, BLOCK_CELLS), NEG)
    mass_weights = mass_weights.reshape(-1, BLOCK_CELLS)
    best = jax.ops.segment_max(peak_value, seg, num_segments=TB + 1)
    lift = jnp.where(flat_valid[:, None], peak_value - best[seg], NEG)
    summed = jax.ops.segment_sum(mass_weights * jnp.exp(lift), seg, num_segments=TB + 1)
    g_pot = EPSILON * log_b - EPSILON * (best[:TB] + jnp.log(summed[:TB])).reshape(NT)
    return f_pot, g_pot
```

```python
import functools

import jax
import jax.numpy as jnp
from jax import lax
from jax.experimental import pallas as pl
from jax.experimental.pallas import tpu as pltpu
from jax.sharding import PartitionSpec as P

MESH = pl.DeviceIdType.MESH
LAT = 32
BC = 256
TBC = 8
KC = 4
SIDE = 4
ROWS = 16
SBD = 4
NOSLOT = 8
NEG = -1e30
EPSILON = 2.0
LOG2E = 1.4426950408889634
LN2 = 0.6931471805599453
KAPPA = LOG2E / EPSILON
OFFSETS = (0, 1, 3, 2)
THERE = (0, 2, 1, 3)
STORED = 3 * SIDE * SBD * KC


def split3(v):
    hi = v.astype(jnp.bfloat16)
    rest = v - hi.astype(jnp.float32)
    mid = rest.astype(jnp.bfloat16)
    low = (rest - mid.astype(jnp.float32)).astype(jnp.bfloat16)
    return hi, mid, low


def bias_rows(first, second):
    row = lax.broadcasted_iota(jnp.int32, (LAT, BC), 0)
    out = jnp.zeros((LAT, BC), jnp.float32)
    for k, v in enumerate(tuple(first) + tuple(second)):
        v = 1.0 if v is None else v.astype(jnp.float32)
        out = jnp.where(row == k, v, out)
    return out.astype(jnp.bfloat16)


def gray(i):
    return i + i // 2 - 2 * (i // 3)


def kernel(
    x_ref, y_ref, la_ref, g_ref, lb_ref, ids_ref, f_ref, gp_ref,
    xg, yg, lag, gg, idg, ids, lhs, rhs, mrow, srow, keep, tile, part, uall, cm, cs, idv, cpart, rpart,
    xs_s, xs_r, ys_s, ys_r, yf_s, yf_r, la_s, la_r, g_s, g_r, id_s, id_r, ex_s, ex_r, cy_s, cy_r, rr_s, rr_r, loc,
):
    row = lax.axis_index("row")
    col = lax.axis_index("col")
    yme, xme = col // SIDE, col % SIDE
    core = row % 2
    half = LAT // 2
    sibling = (row + 1 - 2 * core, col)

    def xpeer(i):
        return (row, yme * SIDE + (xme + OFFSETS[i]) % SIDE)

    def ypeer(i):
        return (row, ((yme + OFFSETS[i]) % SIDE) * SIDE + xme)

    def rpeer(o):
        return ((row + o) % ROWS, col)

    barrier = pltpu.get_barrier_semaphore()
    for i in range(1, SIDE):
        pl.semaphore_signal(barrier, inc=1, device_id=xpeer(i), device_id_type=MESH)
        pl.semaphore_signal(barrier, inc=1, device_id=ypeer(i), device_id_type=MESH)
    for o in range(1, ROWS):
        pl.semaphore_signal(barrier, inc=1, device_id=rpeer(o), device_id_type=MESH)

    xg[0] = x_ref[...]
    yg[0] = y_ref[...]
    lag[xme] = la_ref[...]
    gg[0] = g_ref[...]
    idg[0] = ids_ref[yme]

    rhs[SIDE * TBC] = jnp.concatenate(
        [jnp.zeros((96, BC), jnp.bfloat16)]
        + [bias_rows([None] * 3, [jnp.full((1, BC), NEG, jnp.float32)] + [jnp.zeros((1, BC), jnp.float32)] * 2)]
        + [jnp.zeros((128, BC), jnp.bfloat16)], axis=0)

    def init(b, _):
        mrow[b] = jnp.full((BC, 128), NEG, jnp.float32)
        srow[b] = jnp.zeros((BC, 128), jnp.float32)
        return 0

    lax.fori_loop(0, SIDE * SBD, init, 0)

    pl.semaphore_wait(barrier, 2 * (SIDE - 1) + ROWS - 1)

    def remote(src, dst, s, r, dev):
        return pltpu.make_async_remote_copy(
            src_ref=src, dst_ref=dst, send_sem=s, recv_sem=r, device_id=dev, device_id_type=MESH)

    mine = pl.ds(pl.multiple_of(core * half, half), half)
    theirs = pl.ds(pl.multiple_of((1 - core) * half, half), half)
    sends = []

    def send(src, dst, s, r, dev):
        copy = remote(src, dst, s, r, dev)
        copy.start()
        sends.append(copy)

    for i in range(1, SIDE):
        t = THERE[i]
        send(x_ref, xg.at[t], xs_s.at[t], xs_r.at[t], xpeer(i))
        send(y_ref.at[mine], yg.at[t, mine], ys_s.at[t], ys_r.at[t], ypeer(i))
        send(ids_ref.at[(yme + OFFSETS[i]) % SIDE], idg.at[t], id_s.at[t], id_r.at[t], ypeer(i))
        send(g_ref, gg.at[t], g_s.at[t], g_r.at[t], ypeer(i))
        send(la_ref, lag.at[xme], la_s.at[t], la_r.at[t], xpeer(i))

    def await_x(i):
        remote(x_ref, xg.at[i], xs_s.at[i], xs_r.at[i], sibling).wait_recv()

    def forward_y(i):
        remote(y_ref.at[mine], yg.at[i, mine], ys_s.at[i], ys_r.at[i], sibling).wait_recv()
        remote(yg.at[i, mine], yg.at[i, mine], yf_s.at[i], yf_r.at[i], sibling).start()

    def await_y(i):
        remote(yg.at[i, mine], yg.at[i, theirs], yf_s.at[i], yf_r.at[i], sibling).wait()
        remote(g_ref, gg.at[i], g_s.at[i], g_r.at[i], sibling).wait_recv()
        remote(ids_ref.at[0], idg.at[i], id_s.at[i], id_r.at[i], sibling).wait_recv()

    def prep_x(i):
        def one(b, _):
            v = xg[i, :, pl.ds(pl.multiple_of(b * BC, BC), BC)]
            hi, mid, low = split3(v * KAPPA)
            norm = jnp.sum(v * v, axis=0, keepdims=True) * (-0.5 * KAPPA)
            z = jnp.concatenate(
                [hi, mid, low, bias_rows(split3(norm), [None] * 3), hi, mid, hi, jnp.zeros((LAT, BC), jnp.bfloat16)], axis=0)
            lhs[i * SBD + b] = z.T
            return 0

        lax.fori_loop(0, SBD, one, 0)

    def prep_y(i):
        def one(t, _):
            v = yg[i, :, pl.ds(pl.multiple_of(t * BC, BC), BC)]
            hi, mid, low = split3(v)
            bias = gg[i, pl.ds(t, 1), :] * KAPPA - jnp.sum(v * v, axis=0, keepdims=True) * (0.5 * KAPPA)
            rhs[i * TBC + t] = jnp.concatenate(
                [hi, hi, hi, bias_rows([None] * 3, split3(bias)), mid, mid, low, jnp.zeros((LAT, BC), jnp.bfloat16)], axis=0)
            return 0

        lax.fori_loop(0, TBC, one, 0)
        copy = pltpu.make_async_copy(idg.at[i], ids.at[i], loc)
        copy.start()
        copy.wait()

    def listed(xi, yi, b, k):
        return ids[yi, 0, (((xme + gray(xi)) % SIDE) * SBD + b) * KC + k]

    def score(xi, yi, b, k):
        t = listed(xi, yi, b, k)
        t = jnp.where(t == NOSLOT, SIDE * TBC, yi * TBC + t)
        return jnp.dot(lhs[xi * SBD + b], rhs[t], preferred_element_type=jnp.float32)

    def row_step(xi, yi, kept):
        for b in range(SBD):
            j = xi * SBD + b
            tiles = []
            for k in range(KC):
                v = score(xi, yi, b, k)
                if kept:
                    keep[(yi * SIDE + xi) * SBD * KC + b * KC + k] = v
                tiles.append(v)
            old = mrow[j]
            top = old
            for v in tiles:
                top = jnp.maximum(top, jnp.maximum(v[:, :128], v[:, 128:]))
            total = srow[j] * jnp.exp2(old - top)
            for v in tiles:
                total = total + (jnp.exp2(v[:, :128] - top) + jnp.exp2(v[:, 128:] - top))
            mrow[j] = top
            srow[j] = total

    def first(s, _):
        early = s < 9
        xi = jnp.where(early, s % 3, SIDE - 1)
        yi = jnp.where(early, s // 3, s - 9)

        @pl.when((s == 1) | (s == 2) | (s == 9))
        def _():
            await_x(xi)

        @pl.when(s == 1)
        def _():
            forward_y(1)
            forward_y(2)

        @pl.when(s == 9)
        def _():
            forward_y(3)

        @pl.when((s == 3) | (s == 6))
        def _():
            await_y(yi)

        @pl.when((s < 3) | (s == 9))
        def _():
            prep_x(xi)

        @pl.when((s == 0) | (s == 3) | (s == 6))
        def _():
            prep_y(yi)

        row_step(xi, yi, True)
        return 0

    lax.fori_loop(0, 12, first, 0)
    await_y(3)
    prep_y(3)

    def second(xi, _):
        row_step(xi, SIDE - 1, False)
        return 0

    lax.fori_loop(0, SIDE, second, 0)

    lane = lax.broadcasted_iota(jnp.int32, (BC, 128), 1)
    tile[...] = jnp.zeros((BC, 128), jnp.float32)

    def reduce_rows(j, _):
        m = mrow[j]
        top = jnp.max(m, axis=1, keepdims=True)
        total = jnp.sum(srow[j] * jnp.exp2(m - top), axis=1, keepdims=True)
        place = ((xme + gray(j // SBD)) % SIDE) * SBD + j % SBD
        tile[...] = jnp.where(lane == place, top + jnp.log2(total), tile[...])
        return 0

    lax.fori_loop(0, SIDE * SBD, reduce_rows, 0)
    part[0] = tile[...].T[: SIDE * SBD]

    for i in range(1, SIDE):
        t = THERE[i]
        send(part.at[0], part.at[t], ex_s.at[t], ex_r.at[t], xpeer(i))
    for i in range(1, SIDE):
        remote(part.at[0], part.at[i], ex_s.at[i], ex_r.at[i], sibling).wait_recv()
        remote(la_ref, lag.at[0], la_s.at[i], la_r.at[i], sibling).wait_recv()

    parts = [part[i] for i in range(SIDE)]
    top = functools.reduce(jnp.maximum, parts)
    lse = top + jnp.log2(sum(jnp.exp2(v - top) for v in parts))
    mass = jnp.concatenate([lag[a, :SBD] for a in range(SIDE)], axis=0)
    u = mass * LOG2E - lse
    for a in range(SIDE):
        uall[a] = u[a * SBD:(a + 1) * SBD] * (EPSILON * LN2)
    f_ref[...] = uall[xme]
    tile[...] = jnp.concatenate([u, jnp.zeros((128 - SIDE * SBD, BC), jnp.float32)], axis=0).T

    def spread(j, _):
        place = ((xme + gray(j // SBD)) % SIDE) * SBD + j % SBD
        c = jnp.sum(jnp.where(lane == place, tile[...], 0.0), axis=1, keepdims=True)
        mrow[j] = jnp.broadcast_to(c, (BC, 128))
        return 0

    lax.fori_loop(0, SIDE * SBD, spread, 0)

    def col_step(xi, yi, kept):
        for b in range(SBD):
            for k in range(KC):
                if kept:
                    v = keep.at[(yi * SIDE + xi) * SBD * KC + b * KC + k]
                else:
                    v = score(xi, yi, b, k)
                at = b * KC + k
                for h in range(2):
                    lanes = slice(h * 128, (h + 1) * 128)
                    t = (v[:, lanes] + mrow[xi * SBD + b]).reshape(BC // 8, 8, 128)
                    peak = jnp.max(jnp.max(t, axis=0), axis=0, keepdims=True)
                    total = jnp.sum(jnp.sum(jnp.exp2(t - peak), axis=0), axis=0, keepdims=True)
                    cm[yi * SIDE + xi, at:at + 1, lanes] = peak
                    cs[yi * SIDE + xi, at:at + 1, lanes] = total
                idv[yi * SIDE + xi, at:at + 1, :] = jnp.full((1, BC), listed(xi, yi, b, k), jnp.int32)

    def finish_cols(yi):
        group = pl.ds(yi * SIDE, SIDE)
        for t in range(TBC):
            hit = idv[group] == t
            m = cm[group]
            peak = jnp.max(jnp.where(hit, m, NEG).reshape(-1, BC), axis=0, keepdims=True)
            total = jnp.where(hit, cs[group] * jnp.exp2(m - peak[None]), 0.0)
            total = jnp.sum(total.reshape(-1, BC), axis=0, keepdims=True)
            some = total > 0.0
            cpart[yi, t:t + 1, :] = jnp.where(some, peak + jnp.log2(jnp.where(some, total, 1.0)), NEG)

    def third(xi, _):
        col_step(xi, SIDE - 1, False)
        return 0

    lax.fori_loop(0, SIDE, third, 0)
    finish_cols(SIDE - 1)
    send(cpart.at[3], rpart.at[0, THERE[3]], cy_s.at[3], cy_r.at[THERE[3]], ypeer(3))

    def fourth(yi):
        def body(xi, _):
            col_step(xi, yi, True)
            return 0

        lax.fori_loop(0, SIDE, body, 0)
        finish_cols(yi)

    def fourth_pair(q, _):
        fourth(q)
        return 0

    lax.fori_loop(1, 3, fourth_pair, 0)
    for i in (1, 2):
        send(cpart.at[i], rpart.at[0, THERE[i]], cy_s.at[i], cy_r.at[THERE[i]], ypeer(i))
    fourth(0)

    def join(values):
        peak = functools.reduce(jnp.maximum, values)
        return peak + jnp.log2(sum(jnp.exp2(v - peak) for v in values))

    values = [cpart[0]]
    for i in range(1, SIDE):
        remote(cpart.at[0], rpart.at[0, i], cy_s.at[i], cy_r.at[i], sibling).wait_recv()
        values.append(rpart[0, i])
    own = join(values)
    cpart[4] = own
    for o in range(1, ROWS):
        send(cpart.at[4], rpart.at[1, ROWS - o], rr_s.at[o], rr_r.at[ROWS - o], rpeer(o))
    values = [own]
    for o in range(1, ROWS):
        remote(cpart.at[4], rpart.at[1, o], rr_s.at[o], rr_r.at[o], sibling).wait_recv()
        values.append(rpart[1, o])
    gp_ref[...] = EPSILON * lb_ref[...] - (EPSILON * LN2) * (join(values) - g_ref[...] * KAPPA)
    for copy in sends:
        copy.wait_send()


def per_device(src_emb, tgt_emb, log_a, log_b, g_init, lists, counts):
    blocks = lists.shape[0]
    ids = jnp.where(jnp.arange(KC, dtype=jnp.int32)[None, :] < counts, lists.reshape(blocks, KC), NOSLOT)
    ids = jnp.pad(ids.reshape(SIDE, 1, SIDE * SBD * KC), ((0, 0), (0, 7), (0, 64)))
    la = jnp.pad(log_a.reshape(SBD, BC), ((0, 8 - SBD), (0, 0)))
    f32, bf16 = jnp.float32, jnp.bfloat16
    dma4 = pltpu.SemaphoreType.DMA((SIDE,))
    f, g = pl.pallas_call(
        kernel,
        out_shape=(jax.ShapeDtypeStruct((SBD, BC), f32), jax.ShapeDtypeStruct((TBC, BC), f32)),
        in_specs=[pl.BlockSpec(memory_space=pltpu.VMEM)] * 6,
        out_specs=(pl.BlockSpec(memory_space=pltpu.VMEM),) * 2,
        scratch_shapes=[
            pltpu.VMEM((SIDE, LAT, SBD * BC), f32),
            pltpu.VMEM((SIDE, LAT, TBC * BC), f32),
            pltpu.VMEM((SIDE, 8, BC), f32),
            pltpu.VMEM((SIDE, TBC, BC), f32),
            pltpu.VMEM((SIDE, 8, 128), jnp.int32),
            pltpu.SMEM((SIDE, 8, 128), jnp.int32),
            pltpu.VMEM((SIDE * SBD, BC, 256), bf16),
            pltpu.VMEM((SIDE * TBC + 1, 256, BC), bf16),
            pltpu.VMEM((SIDE * SBD, BC, 128), f32),
            pltpu.VMEM((SIDE * SBD, BC, 128), f32),
            pltpu.VMEM((STORED, BC, BC), f32),
            pltpu.VMEM((BC, 128), f32),
            pltpu.VMEM((SIDE, SIDE * SBD, BC), f32),
            pltpu.VMEM((SIDE, SBD, BC), f32),
            pltpu.VMEM((SIDE * SIDE, SBD * KC, BC), f32),
            pltpu.VMEM((SIDE * SIDE, SBD * KC, BC), f32),
            pltpu.VMEM((SIDE * SIDE, SBD * KC, BC), jnp.int32),
            pltpu.VMEM((SIDE + 1, TBC, BC), f32),
            pltpu.VMEM((2, ROWS, TBC, BC), f32),
        ] + [dma4] * 16 + [pltpu.SemaphoreType.DMA((ROWS,))] * 2 + [pltpu.SemaphoreType.DMA],
        compiler_params=pltpu.CompilerParams(
            collective_id=0, has_side_effects=True, vmem_limit_bytes=63 * 2**20),
        name="sinkhorn",
    )(src_emb, tgt_emb, la, g_init.reshape(TBC, BC), log_b.reshape(TBC, BC), ids)
    return f.reshape(-1), g.reshape(-1)


def solution(mesh):
    in_specs = (
        P(None, ("row", "col")),
        P(None, "col"),
        P(("row", "col")),
        P("col"),
        P("col"),
        P("row", "col", None),
        P("row", "col"),
    )
    return jax.shard_map(
        per_device, mesh=mesh, in_specs=in_specs, out_specs=(P(("row", "col")), P("col")), check_vma=False)
```

```python
import functools

import jax
import jax.numpy as jnp
from jax import lax
from jax.experimental import pallas as pl
from jax.experimental.pallas import tpu as pltpu
from jax.sharding import PartitionSpec as P

MESH = pl.DeviceIdType.MESH
LAT = 32
BC = 256
TBC = 8
KC = 4
SIDE = 4
ROWS = 16
SBD = 4
NOSLOT = 8
NEG = -1e30
EPSILON = 2.0
LOG2E = 1.4426950408889634
LN2 = 0.6931471805599453
KAPPA = LOG2E / EPSILON
OFFSETS = (0, 1, 3, 2)
THERE = (0, 2, 1, 3)
STORED = 3 * SIDE * KC


def split3(v):
    hi = v.astype(jnp.bfloat16)
    rest = v - hi.astype(jnp.float32)
    mid = rest.astype(jnp.bfloat16)
    low = (rest - mid.astype(jnp.float32)).astype(jnp.bfloat16)
    return hi, mid, low


def bias_rows(first, second):
    row = lax.broadcasted_iota(jnp.int32, (LAT, BC), 0)
    out = jnp.zeros((LAT, BC), jnp.float32)
    for k, v in enumerate(tuple(first) + tuple(second)):
        v = 1.0 if v is None else v.astype(jnp.float32)
        out = jnp.where(row == k, v, out)
    return out.astype(jnp.bfloat16)


def gray(i):
    return i + i // 2 - 2 * (i // 3)


def kernel(
    x_ref, y_ref, la_ref, g_ref, lists_ref, counts_ref, f_ref, gp_ref,
    xg, yg, lag, gg, idg, ids, lhs, rhs, m0, m1, m2, m3, s0, s1, s2, s3, k0, k1, k2, k3, part, uall, cm, cs, idv, cpart, rpart,
    xs_s, xs_r, ys_s, ys_r, yf_s, yf_r, la_s, la_r, g_s, g_r, id_s, id_r, cy_s, cy_r, ex_s, ex_r, rr_s, rr_r, loc,
):
    mrow, srow, keep = (m0, m1, m2, m3), (s0, s1, s2, s3), (k0, k1, k2, k3)
    row = lax.axis_index("row")
    col = lax.axis_index("col")
    yme, xme = col // SIDE, col % SIDE
    core = row % 2
    half = LAT // 2
    sibling = (row + 1 - 2 * core, col)

    def xpeer(i):
        return (row, yme * SIDE + (xme + OFFSETS[i]) % SIDE)

    def ypeer(i):
        return (row, ((yme + OFFSETS[i]) % SIDE) * SIDE + xme)

    def zpeer(d):
        return ((row + 2 * d) % ROWS, col)

    barrier = pltpu.get_barrier_semaphore()
    for i in range(1, SIDE):
        pl.semaphore_signal(barrier, inc=1, device_id=xpeer(i), device_id_type=MESH)
        pl.semaphore_signal(barrier, inc=1, device_id=ypeer(i), device_id_type=MESH)
    for d in range(1, ROWS // 2):
        pl.semaphore_signal(barrier, inc=1, device_id=zpeer(d), device_id_type=MESH)
    pl.semaphore_signal(barrier, inc=1, device_id=sibling, device_id_type=MESH)

    xg[0] = x_ref[...]
    yg[0] = y_ref[...]
    lag[xme] = la_ref[...]
    gg[0] = g_ref[...]
    slot = lax.broadcasted_iota(jnp.int32, (KC, ROWS * SBD), 0)
    idg[0] = jnp.full((8, 128), NOSLOT, jnp.int32)
    idg[0, :KC, :ROWS * SBD] = jnp.where(slot < counts_ref[...], lists_ref[...], NOSLOT)

    rhs[SIDE * TBC] = jnp.concatenate(
        [jnp.zeros((96, BC), jnp.bfloat16)]
        + [bias_rows([None] * 3, [jnp.full((1, BC), NEG, jnp.float32)] + [jnp.zeros((1, BC), jnp.float32)] * 2)]
        + [jnp.zeros((128, BC), jnp.bfloat16)], axis=0)

    def init(xi, _):
        for b in range(SBD):
            mrow[b][xi] = jnp.full((BC, 128), NEG, jnp.float32)
            srow[b][xi] = jnp.zeros((BC, 128), jnp.float32)
        return 0

    lax.fori_loop(0, SIDE, init, 0)

    pl.semaphore_wait(barrier, 2 * (SIDE - 1) + ROWS // 2)

    def remote(src, dst, s, r, dev):
        return pltpu.make_async_remote_copy(
            src_ref=src, dst_ref=dst, send_sem=s, recv_sem=r, device_id=dev, device_id_type=MESH)

    mine = pl.ds(pl.multiple_of(core * half, half), half)
    theirs = pl.ds(pl.multiple_of((1 - core) * half, half), half)

    def sends(i):
        t = THERE[i]
        return [
            remote(x_ref, xg.at[t], xs_s.at[t], xs_r.at[t], xpeer(i)),
            remote(y_ref.at[mine], yg.at[t, mine], ys_s.at[t], ys_r.at[t], ypeer(i)),
            remote(idg.at[0], idg.at[t], id_s.at[t], id_r.at[t], ypeer(i)),
            remote(g_ref, gg.at[t], g_s.at[t], g_r.at[t], ypeer(i)),
            remote(la_ref, lag.at[xme], la_s.at[t], la_r.at[t], xpeer(i)),
        ]

    def row_send(i, a):
        return remote(part.at[0, a], part.at[THERE[i], a], ex_s.at[i, a], ex_r.at[THERE[i], a], xpeer(i))

    def col_send(i):
        return remote(cpart.at[i], rpart.at[0, THERE[i]], cy_s.at[i], cy_r.at[THERE[i]], ypeer(i))

    def pair_send():
        return remote(cpart.at[SIDE], rpart.at[1, 0], rr_s.at[0], rr_r.at[0], sibling)

    def last_send(d):
        return remote(cpart.at[SIDE + 1], rpart.at[1, ROWS // 2 - d], rr_s.at[d], rr_r.at[ROWS // 2 - d], zpeer(d))

    for i in (1, 2):
        for copy in sends(i):
            copy.start()

    def await_x(i):
        remote(x_ref, xg.at[i], xs_s.at[i], xs_r.at[i], sibling).wait_recv()

    def forward_y(i):
        remote(y_ref.at[mine], yg.at[i, mine], ys_s.at[i], ys_r.at[i], sibling).wait_recv()
        remote(yg.at[i, mine], yg.at[i, mine], yf_s.at[i], yf_r.at[i], sibling).start()

    def await_y(i):
        remote(yg.at[i, mine], yg.at[i, theirs], yf_s.at[i], yf_r.at[i], sibling).wait()
        remote(g_ref, gg.at[i], g_s.at[i], g_r.at[i], sibling).wait_recv()
        remote(idg.at[0], idg.at[i], id_s.at[i], id_r.at[i], sibling).wait_recv()

    def prep_x(i):
        def one(b, _):
            v = xg[i, :, pl.ds(pl.multiple_of(b * BC, BC), BC)]
            hi, mid, low = split3(v * KAPPA)
            norm = jnp.sum(v * v, axis=0, keepdims=True) * (-0.5 * KAPPA)
            z = jnp.concatenate(
                [hi, mid, low, bias_rows(split3(norm), [None] * 3), hi, mid, hi, jnp.zeros((LAT, BC), jnp.bfloat16)], axis=0)
            lhs[i * SBD + b] = z.T
            return 0

        lax.fori_loop(0, SBD, one, 0)

    def prep_y(i):
        def one(t, _):
            v = yg[i, :, pl.ds(pl.multiple_of(t * BC, BC), BC)]
            hi, mid, low = split3(v)
            bias = jnp.concatenate([gg[i, pl.ds(2 * t, 1), :], gg[i, pl.ds(2 * t + 1, 1), :]], axis=1) * KAPPA - jnp.sum(v * v, axis=0, keepdims=True) * (0.5 * KAPPA)
            rhs[i * TBC + t] = jnp.concatenate(
                [hi, hi, hi, bias_rows([None] * 3, split3(bias)), mid, mid, low, jnp.zeros((LAT, BC), jnp.bfloat16)], axis=0)
            return 0

        lax.fori_loop(0, TBC, one, 0)
        copy = pltpu.make_async_copy(idg.at[i], ids.at[i], loc)
        copy.start()
        copy.wait()

    def listed(xi, yi, b, k):
        return ids[yi, k, (yme * SIDE + (xme + gray(xi)) % SIDE) * SBD + b]

    def score(xi, yi, b, k):
        t = listed(xi, yi, b, k)
        t = jnp.where(t == NOSLOT, SIDE * TBC, yi * TBC + t)
        return jnp.dot(lhs[xi * SBD + b], rhs[t], preferred_element_type=jnp.float32)

    def row_step(xi, yi, kept):
        tops, tiles = {}, {}

        def scores(b):
            top = mrow[b][xi]
            for k in range(KC):
                v = score(xi, yi, b, k)
                if kept:
                    keep[b][(yi * SIDE + xi) * KC + k] = v
                    v = keep[b].at[(yi * SIDE + xi) * KC + k]
                top = jnp.maximum(top, jnp.maximum(v[:, :128], v[:, 128:]))
                tiles[b, k] = v
            tops[b] = top

        def sums(b):
            top = tops[b]
            total = srow[b][xi] * jnp.exp2(mrow[b][xi] - top)
            for k in range(KC):
                v = tiles[b, k]
                total = total + (jnp.exp2(v[:, :128] - top) + jnp.exp2(v[:, 128:] - top))
            mrow[b][xi] = top
            srow[b][xi] = total

        for b in range(SBD):
            scores(b)
            sums(b)

    def first(s, _):
        early = s < 9
        xi = jnp.where(early, s % 3, SIDE - 1)
        yi = jnp.where(early, s // 3, s - 9)

        @pl.when((s == 1) | (s == 2) | (s == 9))
        def _():
            await_x(xi)

        @pl.when(s == 1)
        def _():
            for copy in sends(3):
                copy.start()
            forward_y(1)
            forward_y(2)

        @pl.when(s == 9)
        def _():
            forward_y(3)

        @pl.when((s == 3) | (s == 6))
        def _():
            await_y(yi)

        @pl.when((s < 3) | (s == 9))
        def _():
            prep_x(xi)

        @pl.when((s == 0) | (s == 3) | (s == 6))
        def _():
            prep_y(yi)

        row_step(xi, yi, True)
        return 0

    lax.fori_loop(0, 12, first, 0)
    await_y(3)
    prep_y(3)

    lane = lax.broadcasted_iota(jnp.int32, (BC, 128), 1)

    def second(a, _):
        xi = gray((a - xme + SIDE) % SIDE)
        row_step(xi, SIDE - 1, False)
        out = jnp.zeros((BC, 128), jnp.float32)
        for b in range(SBD):
            m = mrow[b][xi]
            top = jnp.max(m, axis=1, keepdims=True)
            total = jnp.sum(srow[b][xi] * jnp.exp2(m - top), axis=1, keepdims=True)
            out = jnp.where(lane == b, top + jnp.log2(total), out)
        part[0, a] = out.T[:8]
        for i in range(1, SIDE):
            row_send(i, a).start()
        return 0

    lax.fori_loop(0, SIDE, second, 0)
    for i in range(1, SIDE):
        remote(la_ref, lag.at[0], la_s.at[i], la_r.at[i], sibling).wait_recv()

    def potential(a):
        xi = gray((a - xme + SIDE) % SIDE)
        parts = [part[0, a]]
        for i in range(1, SIDE):
            remote(part.at[0, a], part.at[i, a], ex_s.at[i, a], ex_r.at[i, a], sibling).wait_recv()
            parts.append(part[i, a])
        top = functools.reduce(jnp.maximum, parts)
        lse = top + jnp.log2(sum(jnp.exp2(v - top) for v in parts))
        mass = jnp.concatenate(
            [jnp.concatenate([lag[a, 2 * b:2 * b + 1], lag[a, 2 * b + 1:2 * b + 2]], axis=1) for b in range(SBD)]
            + [jnp.zeros((8 - SBD, BC), jnp.float32)], axis=0)
        u = mass * LOG2E - lse
        for b in range(SBD):
            for h in range(2):
                uall[a, 2 * b + h:2 * b + h + 1, :] = u[b:b + 1, h * 128:(h + 1) * 128]
        across = jnp.concatenate([u, jnp.zeros((120, BC), jnp.float32)], axis=0).T
        for b in range(SBD):
            mrow[b][xi] = jnp.broadcast_to(across[:, b:b + 1], (BC, 128))
        return xi

    def col_step(xi, yi, kept):
        for b in range(SBD):
            for k in range(KC):
                if kept:
                    v = keep[b].at[(yi * SIDE + xi) * KC + k]
                else:
                    v = score(xi, yi, b, k)
                at = b * KC + k
                for h in range(2):
                    lanes = slice(h * 128, (h + 1) * 128)
                    t = (v[:, lanes] + mrow[b][xi]).reshape(BC // 8, 8, 128)
                    peak = jnp.max(jnp.max(t, axis=0), axis=0, keepdims=True)
                    total = jnp.sum(jnp.sum(jnp.exp2(t - peak), axis=0), axis=0, keepdims=True)
                    cm[yi * SIDE + xi, at:at + 1, lanes] = peak
                    cs[yi * SIDE + xi, at:at + 1, lanes] = total
                idv[yi * SIDE + xi, at:at + 1, :] = jnp.full((1, BC), listed(xi, yi, b, k), jnp.int32)

    def finish_cols(yi):
        group = pl.ds(yi * SIDE, SIDE)
        for t in range(TBC):
            hit = idv[group] == t
            m = cm[group]
            peak = jnp.max(jnp.where(hit, m, NEG).reshape(-1, BC), axis=0, keepdims=True)
            total = jnp.where(hit, cs[group] * jnp.exp2(m - peak[None]), 0.0)
            total = jnp.sum(total.reshape(-1, BC), axis=0, keepdims=True)
            some = total > 0.0
            value = jnp.where(some, peak + jnp.log2(jnp.where(some, total, 1.0)), NEG)
            for h in range(2):
                cpart[yi, 2 * t + h:2 * t + h + 1, :] = value[:, h * 128:(h + 1) * 128]

    def third(a, _):
        col_step(potential(a), SIDE - 1, False)
        return 0

    lax.fori_loop(0, SIDE, third, 0)
    f_ref[...] = uall[xme]
    finish_cols(SIDE - 1)
    col_send(3).start()

    def fourth(yi):
        def body(xi, _):
            col_step(xi, yi, True)
            return 0

        lax.fori_loop(0, SIDE, body, 0)
        finish_cols(yi)

    def fourth_pair(q, _):
        fourth(q)
        return 0

    lax.fori_loop(1, 3, fourth_pair, 0)
    for i in (1, 2):
        col_send(i).start()
    fourth(0)

    def join(values):
        peak = functools.reduce(jnp.maximum, values)
        return peak + jnp.log2(sum(jnp.exp2(v - peak) for v in values))

    values = [cpart[0]]
    for i in range(1, SIDE):
        remote(cpart.at[0], rpart.at[0, i], cy_s.at[i], cy_r.at[i], sibling).wait_recv()
        values.append(rpart[0, i])
    cpart[SIDE] = join(values)
    pair_send().start()
    remote(cpart.at[SIDE], rpart.at[1, 0], rr_s.at[0], rr_r.at[0], sibling).wait_recv()
    both = join([cpart[SIDE], rpart[1, 0]])
    cpart[SIDE + 1] = both
    for d in range(1, ROWS // 2):
        last_send(d).start()
    values = [both]
    for d in range(1, ROWS // 2):
        remote(cpart.at[SIDE], rpart.at[1, d], rr_s.at[d], rr_r.at[d], sibling).wait_recv()
        values.append(rpart[1, d])
    gp_ref[...] = join(values)
    for i in range(1, SIDE):
        for copy in sends(i) + [col_send(i)] + [row_send(i, a) for a in range(SIDE)]:
            copy.wait_send()
    pair_send().wait_send()
    for d in range(1, ROWS // 2):
        last_send(d).wait_send()


def per_device(src_emb, tgt_emb, log_a, log_b, g_init, lists, counts):
    f32, bf16 = jnp.float32, jnp.bfloat16
    dma4 = pltpu.SemaphoreType.DMA((SIDE,))
    u, lse = pl.pallas_call(
        kernel,
        out_shape=(jax.ShapeDtypeStruct((8, 128), f32), jax.ShapeDtypeStruct((16, 128), f32)),
        in_specs=[pl.BlockSpec(memory_space=pltpu.VMEM)] * 6,
        out_specs=(pl.BlockSpec(memory_space=pltpu.VMEM),) * 2,
        scratch_shapes=[
            pltpu.VMEM((SIDE, LAT, SBD * BC), f32),
            pltpu.VMEM((SIDE, LAT, TBC * BC), f32),
            pltpu.VMEM((SIDE, 8, 128), f32),
            pltpu.VMEM((SIDE, 16, 128), f32),
            pltpu.VMEM((SIDE, 8, 128), jnp.int32),
            pltpu.SMEM((SIDE, 8, 128), jnp.int32),
            pltpu.VMEM((SIDE * SBD, BC, 256), bf16),
            pltpu.VMEM((SIDE * TBC + 1, 256, BC), bf16),
        ] + [pltpu.VMEM((SIDE, BC, 128), f32)] * (2 * SBD) + [pltpu.VMEM((STORED, BC, BC), f32)] * SBD + [
            pltpu.VMEM((SIDE, SIDE, 8, BC), f32),
            pltpu.VMEM((SIDE, 8, 128), f32),
            pltpu.VMEM((SIDE * SIDE, SBD * KC, BC), f32),
            pltpu.VMEM((SIDE * SIDE, SBD * KC, BC), f32),
            pltpu.VMEM((SIDE * SIDE, SBD * KC, BC), jnp.int32),
            pltpu.VMEM((SIDE + 2, 16, 128), f32),
            pltpu.VMEM((2, ROWS, 16, 128), f32),
        ] + [dma4] * 14 + [pltpu.SemaphoreType.DMA((SIDE, SIDE))] * 2 + [pltpu.SemaphoreType.DMA((ROWS // 2,))] * 2 + [pltpu.SemaphoreType.DMA],
        compiler_params=pltpu.CompilerParams(
            collective_id=0, has_side_effects=True, vmem_limit_bytes=63 * 2**20),
        name="sinkhorn",
    )(src_emb, tgt_emb, log_a.reshape(8, 128), g_init.reshape(16, 128),
      lists.transpose(1, 2, 0).reshape(KC, ROWS * SBD), counts.reshape(1, ROWS * SBD))
    f = u.reshape(-1) * (EPSILON * LN2)
    g = EPSILON * log_b - (EPSILON * LN2) * (lse.reshape(-1) - g_init * KAPPA)
    return f, g


def solution(mesh):
    in_specs = (
        P(None, ("row", "col")),
        P(None, "col"),
        P(("row", "col")),
        P("col"),
        P("col"),
        P("row", "col", None),
        P("row", "col"),
    )
    return jax.shard_map(
        per_device, mesh=mesh, in_specs=in_specs, out_specs=(P(("row", "col")), P("col")), check_vma=False)
```

```python
import functools

import jax
import jax.numpy as jnp
from jax import lax
from jax.experimental import pallas as pl
from jax.experimental.pallas import tpu as pltpu
from jax.sharding import PartitionSpec as P

MESH = pl.DeviceIdType.MESH
LAT = 32
BC = 256
TBC = 8
KC = 4
SIDE = 4
ROWS = 16
SBD = 4
NOSLOT = 8
NEG = -1e30
EPSILON = 2.0
LOG2E = 1.4426950408889634
LN2 = 0.6931471805599453
KAPPA = LOG2E / EPSILON
OFFSETS = (0, 1, 3, 2)
THERE = (0, 2, 1, 3)
STORED = 3 * SIDE * KC


def split3(v):
    hi = v.astype(jnp.bfloat16)
    rest = v - hi.astype(jnp.float32)
    mid = rest.astype(jnp.bfloat16)
    low = (rest - mid.astype(jnp.float32)).astype(jnp.bfloat16)
    return hi, mid, low


def bias_rows(first, second):
    row = lax.broadcasted_iota(jnp.int32, (LAT, BC), 0)
    out = jnp.zeros((LAT, BC), jnp.float32)
    for k, v in enumerate(tuple(first) + tuple(second)):
        v = 1.0 if v is None else v.astype(jnp.float32)
        out = jnp.where(row == k, v, out)
    return out.astype(jnp.bfloat16)


def gray(i):
    return i + i // 2 - 2 * (i // 3)


def kernel(
    x_ref, y_ref, la_ref, g_ref, lists_ref, counts_ref, f_ref, gp_ref,
    xg, yg, lag, gg, idg, ids, lhs, rhs, m0, m1, m2, m3, s0, s1, s2, s3, k0, k1, k2, k3, part, uall, cm, cs, idv, cpart, rpart,
    xs_s, xs_r, ys_s, ys_r, yf_s, yf_r, la_s, la_r, g_s, g_r, id_s, id_r, cy_s, cy_r, ex_s, ex_r, rr_s, rr_r, loc,
):
    mrow, srow, keep = (m0, m1, m2, m3), (s0, s1, s2, s3), (k0, k1, k2, k3)
    row = lax.axis_index("row")
    col = lax.axis_index("col")
    yme, xme = col // SIDE, col % SIDE
    core = row % 2
    half = LAT // 2
    sibling = (row + 1 - 2 * core, col)

    def xpeer(i):
        return (row, yme * SIDE + (xme + OFFSETS[i]) % SIDE)

    def ypeer(i):
        return (row, ((yme + OFFSETS[i]) % SIDE) * SIDE + xme)

    def zpeer(d):
        return ((row + 2 * d) % ROWS, col)

    barrier = pltpu.get_barrier_semaphore()
    for i in range(1, SIDE):
        pl.semaphore_signal(barrier, inc=1, device_id=xpeer(i), device_id_type=MESH)
        pl.semaphore_signal(barrier, inc=1, device_id=ypeer(i), device_id_type=MESH)
    for d in range(1, ROWS // 2):
        pl.semaphore_signal(barrier, inc=1, device_id=zpeer(d), device_id_type=MESH)
    pl.semaphore_signal(barrier, inc=1, device_id=sibling, device_id_type=MESH)

    xg[0] = x_ref[...]
    yg[0] = y_ref[...]
    lag[xme] = la_ref[...]
    gg[0] = g_ref[...]
    slot = lax.broadcasted_iota(jnp.int32, (KC, ROWS * SBD), 0)
    idg[0] = jnp.full((8, 128), NOSLOT, jnp.int32)
    idg[0, :KC, :ROWS * SBD] = jnp.where(slot < counts_ref[...], lists_ref[...], NOSLOT)

    rhs[SIDE * TBC] = jnp.concatenate(
        [jnp.zeros((96, BC), jnp.bfloat16)]
        + [bias_rows([None] * 3, [jnp.full((1, BC), NEG, jnp.float32)] + [jnp.zeros((1, BC), jnp.float32)] * 2)]
        + [jnp.zeros((128, BC), jnp.bfloat16)], axis=0)

    def init(xi, _):
        for b in range(SBD):
            mrow[b][xi] = jnp.full((BC, 128), NEG, jnp.float32)
            srow[b][xi] = jnp.zeros((BC, 128), jnp.float32)
        return 0

    lax.fori_loop(0, SIDE, init, 0)

    pl.semaphore_wait(barrier, 2 * (SIDE - 1) + ROWS // 2)

    def remote(src, dst, s, r, dev):
        return pltpu.make_async_remote_copy(
            src_ref=src, dst_ref=dst, send_sem=s, recv_sem=r, device_id=dev, device_id_type=MESH)

    mine = pl.ds(pl.multiple_of(core * half, half), half)
    theirs = pl.ds(pl.multiple_of((1 - core) * half, half), half)

    def sends(i):
        t = THERE[i]
        return [
            remote(x_ref, xg.at[t], xs_s.at[t], xs_r.at[t], xpeer(i)),
            remote(y_ref.at[mine], yg.at[t, mine], ys_s.at[t], ys_r.at[t], ypeer(i)),
            remote(idg.at[0], idg.at[t], id_s.at[t], id_r.at[t], ypeer(i)),
            remote(g_ref, gg.at[t], g_s.at[t], g_r.at[t], ypeer(i)),
            remote(la_ref, lag.at[xme], la_s.at[t], la_r.at[t], xpeer(i)),
        ]

    def row_send(i, a):
        return remote(part.at[0, a], part.at[THERE[i], a], ex_s.at[i, a], ex_r.at[THERE[i], a], xpeer(i))

    def col_send(i):
        return remote(cpart.at[i], rpart.at[0, THERE[i]], cy_s.at[i], cy_r.at[THERE[i]], ypeer(i))

    def pair_send():
        return remote(cpart.at[SIDE], rpart.at[1, 0], rr_s.at[0], rr_r.at[0], sibling)

    def last_send(d):
        return remote(cpart.at[SIDE + 1], rpart.at[1, ROWS // 2 - d], rr_s.at[d], rr_r.at[ROWS // 2 - d], zpeer(d))

    for i in (1, 2):
        for copy in sends(i):
            copy.start()

    def await_x(i):
        remote(x_ref, xg.at[i], xs_s.at[i], xs_r.at[i], sibling).wait_recv()

    def forward_y(i):
        remote(y_ref.at[mine], yg.at[i, mine], ys_s.at[i], ys_r.at[i], sibling).wait_recv()
        remote(yg.at[i, mine], yg.at[i, mine], yf_s.at[i], yf_r.at[i], sibling).start()

    def await_y(i):
        remote(yg.at[i, mine], yg.at[i, theirs], yf_s.at[i], yf_r.at[i], sibling).wait()
        remote(g_ref, gg.at[i], g_s.at[i], g_r.at[i], sibling).wait_recv()
        remote(idg.at[0], idg.at[i], id_s.at[i], id_r.at[i], sibling).wait_recv()

    def prep_x(i):
        def one(b, _):
            v = xg[i, :, pl.ds(pl.multiple_of(b * BC, BC), BC)]
            hi, mid, low = split3(v * KAPPA)
            norm = jnp.sum(v * v, axis=0, keepdims=True) * (-0.5 * KAPPA)
            z = jnp.concatenate(
                [hi, mid, low, bias_rows(split3(norm), [None] * 3), hi, mid, hi, jnp.zeros((LAT, BC), jnp.bfloat16)], axis=0)
            lhs[i * SBD + b] = z.T
            return 0

        lax.fori_loop(0, SBD, one, 0)

    def prep_y(i):
        def one(t, _):
            v = yg[i, :, pl.ds(pl.multiple_of(t * BC, BC), BC)]
            hi, mid, low = split3(v)
            bias = jnp.concatenate([gg[i, pl.ds(2 * t, 1), :], gg[i, pl.ds(2 * t + 1, 1), :]], axis=1) * KAPPA - jnp.sum(v * v, axis=0, keepdims=True) * (0.5 * KAPPA)
            rhs[i * TBC + t] = jnp.concatenate(
                [hi, hi, hi, bias_rows([None] * 3, split3(bias)), mid, mid, low, jnp.zeros((LAT, BC), jnp.bfloat16)], axis=0)
            return 0

        lax.fori_loop(0, TBC, one, 0)
        copy = pltpu.make_async_copy(idg.at[i], ids.at[i], loc)
        copy.start()
        copy.wait()

    def listed(xi, yi, b, k):
        return ids[yi, k, (yme * SIDE + (xme + gray(xi)) % SIDE) * SBD + b]

    def score(xi, yi, b, k):
        t = listed(xi, yi, b, k)
        t = jnp.where(t == NOSLOT, SIDE * TBC, yi * TBC + t)
        return jnp.dot(lhs[xi * SBD + b], rhs[t], preferred_element_type=jnp.float32)

    def row_step(xi, yi, kept):
        tops, tiles = {}, {}

        def scores(b):
            top = mrow[b][xi]
            for k in range(KC):
                v = score(xi, yi, b, k)
                if kept:
                    keep[b][(yi * SIDE + xi) * KC + k] = v
                    v = keep[b].at[(yi * SIDE + xi) * KC + k]
                top = jnp.maximum(top, jnp.maximum(v[:, :128], v[:, 128:]))
                tiles[b, k] = v
            tops[b] = top

        def sums(b):
            top = tops[b]
            total = srow[b][xi] * jnp.exp2(mrow[b][xi] - top)
            for k in range(KC):
                v = tiles[b, k]
                total = total + (jnp.exp2(v[:, :128] - top) + jnp.exp2(v[:, 128:] - top))
            mrow[b][xi] = top
            srow[b][xi] = total

        for b in range(SBD):
            scores(b)
            sums(b)

    def first(s, _):
        early = s < 9
        xi = jnp.where(early, s % 3, SIDE - 1)
        yi = jnp.where(early, s // 3, s - 9)

        @pl.when((s == 1) | (s == 2) | (s == 9))
        def _():
            await_x(xi)

        @pl.when(s == 1)
        def _():
            for copy in sends(3):
                copy.start()
            forward_y(1)
            forward_y(2)

        @pl.when(s == 9)
        def _():
            forward_y(3)

        @pl.when((s == 3) | (s == 6))
        def _():
            await_y(yi)

        @pl.when((s < 3) | (s == 9))
        def _():
            prep_x(xi)

        @pl.when((s == 0) | (s == 3) | (s == 6))
        def _():
            prep_y(yi)

        row_step(xi, yi, True)
        return 0

    lax.fori_loop(0, 12, first, 0)
    await_y(3)
    prep_y(3)

    lane = lax.broadcasted_iota(jnp.int32, (BC, 128), 1)

    def second(a, _):
        xi = gray((a - xme + SIDE) % SIDE)
        row_step(xi, SIDE - 1, False)
        out = jnp.zeros((BC, 128), jnp.float32)
        for b in range(SBD):
            m = mrow[b][xi]
            top = jnp.max(m, axis=1, keepdims=True)
            total = jnp.sum(srow[b][xi] * jnp.exp2(m - top), axis=1, keepdims=True)
            out = jnp.where(lane == b, top + jnp.log2(total), out)
        part[0, a] = out.T[:8]
        for i in range(1, SIDE):
            row_send(i, a).start()
        return 0

    lax.fori_loop(0, SIDE, second, 0)
    for i in range(1, SIDE):
        remote(la_ref, lag.at[0], la_s.at[i], la_r.at[i], sibling).wait_recv()

    def potential(a):
        xi = gray((a - xme + SIDE) % SIDE)
        parts = [part[0, a]]
        for i in range(1, SIDE):
            remote(part.at[0, a], part.at[i, a], ex_s.at[i, a], ex_r.at[i, a], sibling).wait_recv()
            parts.append(part[i, a])
        top = functools.reduce(jnp.maximum, parts)
        lse = top + jnp.log2(sum(jnp.exp2(v - top) for v in parts))
        mass = jnp.concatenate(
            [jnp.concatenate([lag[a, 2 * b:2 * b + 1], lag[a, 2 * b + 1:2 * b + 2]], axis=1) for b in range(SBD)]
            + [jnp.zeros((8 - SBD, BC), jnp.float32)], axis=0)
        u = mass * LOG2E - lse
        for b in range(SBD):
            for h in range(2):
                uall[a, 2 * b + h:2 * b + h + 1, :] = u[b:b + 1, h * 128:(h + 1) * 128]
        across = jnp.concatenate([u, jnp.zeros((120, BC), jnp.float32)], axis=0).T
        for b in range(SBD):
            mrow[b][xi] = jnp.broadcast_to(across[:, b:b + 1], (BC, 128))
        return xi

    def col_step(xi, yi, kept):
        for b in range(SBD):
            vs = []
            for k in range(KC):
                vs.append(keep[b].at[(yi * SIDE + xi) * KC + k] if kept else score(xi, yi, b, k))
                idv[yi * SIDE + xi, b * KC + k:b * KC + k + 1, :] = jnp.full((1, BC), listed(xi, yi, b, k), jnp.int32)
            for h in range(2):
                lanes = slice(h * 128, (h + 1) * 128)
                ps = [[] for _ in range(KC)]
                ts = [[] for _ in range(KC)]
                for r in range(0, BC, 64):
                    rows = slice(r, r + 64)
                    u = mrow[b][xi, rows]
                    for k in range(KC):
                        t = (vs[k][rows, lanes] + u).reshape(64 // 8, 8, 128)
                        p = jnp.max(t, axis=0)
                        ps[k].append(p)
                        ts[k].append(jnp.sum(jnp.exp2(t - p), axis=0))
                for k in range(KC):
                    at = b * KC + k
                    m8 = functools.reduce(jnp.maximum, ps[k])
                    peak = jnp.max(m8, axis=0, keepdims=True)
                    total = sum(q * jnp.exp2(p - peak) for q, p in zip(ts[k], ps[k]))
                    cm[yi * SIDE + xi, at:at + 1, lanes] = peak
                    cs[yi * SIDE + xi, at:at + 1, lanes] = jnp.sum(total, axis=0, keepdims=True)

    def finish_cols(yi):
        group = pl.ds(yi * SIDE, SIDE)
        ids_v = idv[group].reshape(-1, BC)
        m = cm[group].reshape(-1, BC)
        c = cs[group].reshape(-1, BC)
        peaks, totals = [], []
        for t in range(TBC):
            hit = ids_v == t
            peak = jnp.max(jnp.where(hit, m, NEG), axis=0, keepdims=True)
            peaks.append(peak)
            totals.append(jnp.sum(jnp.where(hit, c * jnp.exp2(m - peak), 0.0), axis=0, keepdims=True))
        peak = jnp.concatenate(peaks, axis=0)
        total = jnp.concatenate(totals, axis=0)
        some = total > 0.0
        value = jnp.where(some, peak + jnp.log2(jnp.where(some, total, 1.0)), NEG)
        for t in range(TBC):
            for h in range(2):
                cpart[yi, 2 * t + h:2 * t + h + 1, :] = value[t:t + 1, h * 128:(h + 1) * 128]

    def third(a, _):
        col_step(potential(a), SIDE - 1, False)
        return 0

    lax.fori_loop(0, SIDE, third, 0)
    f_ref[...] = uall[xme]
    finish_cols(SIDE - 1)
    col_send(3).start()

    def fourth(yi):
        def body(xi, _):
            col_step(xi, yi, True)
            return 0

        lax.fori_loop(0, SIDE, body, 0)
        finish_cols(yi)

    def fourth_pair(q, _):
        fourth(q)
        return 0

    lax.fori_loop(1, 3, fourth_pair, 0)
    for i in (1, 2):
        col_send(i).start()
    fourth(0)

    def join(values):
        peak = functools.reduce(jnp.maximum, values)
        return peak + jnp.log2(sum(jnp.exp2(v - peak) for v in values))

    values = [cpart[0]]
    for i in range(1, SIDE):
        remote(cpart.at[0], rpart.at[0, i], cy_s.at[i], cy_r.at[i], sibling).wait_recv()
        values.append(rpart[0, i])
    cpart[SIDE] = join(values)
    pair_send().start()
    remote(cpart.at[SIDE], rpart.at[1, 0], rr_s.at[0], rr_r.at[0], sibling).wait_recv()
    both = join([cpart[SIDE], rpart[1, 0]])
    cpart[SIDE + 1] = both
    for d in range(1, ROWS // 2):
        last_send(d).start()
    values = [both]
    for d in range(1, ROWS // 2):
        remote(cpart.at[SIDE], rpart.at[1, d], rr_s.at[d], rr_r.at[d], sibling).wait_recv()
        values.append(rpart[1, d])
    gp_ref[...] = join(values)
    for i in range(1, SIDE):
        for copy in sends(i) + [col_send(i)] + [row_send(i, a) for a in range(SIDE)]:
            copy.wait_send()
    pair_send().wait_send()
    for d in range(1, ROWS // 2):
        last_send(d).wait_send()


def finish(u_ref, lse_ref, g_ref, lb_ref, f_ref, gp_ref):
    f_ref[...] = u_ref[...] * (EPSILON * LN2)
    gp_ref[...] = EPSILON * lb_ref[...] - (EPSILON * LN2) * (lse_ref[...] - g_ref[...] * KAPPA)


def per_device(src_emb, tgt_emb, log_a, log_b, g_init, lists, counts):
    f32, bf16 = jnp.float32, jnp.bfloat16
    dma4 = pltpu.SemaphoreType.DMA((SIDE,))
    u, lse = pl.pallas_call(
        kernel,
        out_shape=(jax.ShapeDtypeStruct((8, 128), f32), jax.ShapeDtypeStruct((16, 128), f32)),
        in_specs=[pl.BlockSpec(memory_space=pltpu.VMEM)] * 6,
        out_specs=(pl.BlockSpec(memory_space=pltpu.VMEM),) * 2,
        scratch_shapes=[
            pltpu.VMEM((SIDE, LAT, SBD * BC), f32),
            pltpu.VMEM((SIDE, LAT, TBC * BC), f32),
            pltpu.VMEM((SIDE, 8, 128), f32),
            pltpu.VMEM((SIDE, 16, 128), f32),
            pltpu.VMEM((SIDE, 8, 128), jnp.int32),
            pltpu.SMEM((SIDE, 8, 128), jnp.int32),
            pltpu.VMEM((SIDE * SBD, BC, 256), bf16),
            pltpu.VMEM((SIDE * TBC + 1, 256, BC), bf16),
        ] + [pltpu.VMEM((SIDE, BC, 128), f32)] * (2 * SBD) + [pltpu.VMEM((STORED, BC, BC), f32)] * SBD + [
            pltpu.VMEM((SIDE, SIDE, 8, BC), f32),
            pltpu.VMEM((SIDE, 8, 128), f32),
            pltpu.VMEM((SIDE * SIDE, SBD * KC, BC), f32),
            pltpu.VMEM((SIDE * SIDE, SBD * KC, BC), f32),
            pltpu.VMEM((SIDE * SIDE, SBD * KC, BC), jnp.int32),
            pltpu.VMEM((SIDE + 2, 16, 128), f32),
            pltpu.VMEM((2, ROWS, 16, 128), f32),
        ] + [dma4] * 14 + [pltpu.SemaphoreType.DMA((SIDE, SIDE))] * 2 + [pltpu.SemaphoreType.DMA((ROWS // 2,))] * 2 + [pltpu.SemaphoreType.DMA],
        compiler_params=pltpu.CompilerParams(
            collective_id=0, has_side_effects=True, vmem_limit_bytes=63 * 2**20),
        name="sinkhorn",
    )(src_emb, tgt_emb, log_a.reshape(8, 128), g_init.reshape(16, 128),
      lists.transpose(1, 2, 0).reshape(KC, ROWS * SBD), counts.reshape(1, ROWS * SBD))
    f, g = pl.pallas_call(
        finish,
        out_shape=(jax.ShapeDtypeStruct((8, 128), f32), jax.ShapeDtypeStruct((16, 128), f32)),
        in_specs=[pl.BlockSpec(memory_space=pltpu.VMEM)] * 4,
        out_specs=(pl.BlockSpec(memory_space=pltpu.VMEM),) * 2,
        name="finish",
    )(u, lse, g_init.reshape(16, 128), log_b.reshape(16, 128))
    return f.reshape(-1), g.reshape(-1)


def solution(mesh):
    in_specs = (
        P(None, ("row", "col")),
        P(None, "col"),
        P(("row", "col")),
        P("col"),
        P("col"),
        P("row", "col", None),
        P("row", "col"),
    )
    return jax.shard_map(
        per_device, mesh=mesh, in_specs=in_specs, out_specs=(P(("row", "col")), P("col")), check_vma=False)
```

```python
import functools

import jax
import jax.numpy as jnp
from jax import lax
from jax.experimental import pallas as pl
from jax.experimental.pallas import tpu as pltpu
from jax.sharding import PartitionSpec as P

MESH = pl.DeviceIdType.MESH
LAT = 32
BC = 256
TBC = 8
KC = 4
SIDE = 4
ROWS = 16
SBD = 4
NOSLOT = 8
NEG = -1e30
EPSILON = 2.0
LOG2E = 1.4426950408889634
LN2 = 0.6931471805599453
KAPPA = LOG2E / EPSILON
OFFSETS = (0, 1, 3, 2)
THERE = (0, 2, 1, 3)
STORED = 3 * SIDE * KC


def split3(v):
    hi = v.astype(jnp.bfloat16)
    rest = v - hi.astype(jnp.float32)
    mid = rest.astype(jnp.bfloat16)
    low = (rest - mid.astype(jnp.float32)).astype(jnp.bfloat16)
    return hi, mid, low


def bias_rows(first, second):
    row = lax.broadcasted_iota(jnp.int32, (LAT, BC), 0)
    out = jnp.zeros((LAT, BC), jnp.float32)
    for k, v in enumerate(tuple(first) + tuple(second)):
        v = 1.0 if v is None else v.astype(jnp.float32)
        out = jnp.where(row == k, v, out)
    return out.astype(jnp.bfloat16)


def gray(i):
    return i + i // 2 - 2 * (i // 3)


def kernel(
    x_ref, y_ref, la_ref, g_ref, lists_ref, counts_ref, f_ref, gp_ref,
    xg, yg, lag, gg, idg, ids, lhs, rhs, m0, m1, m2, m3, s0, s1, s2, s3, k0, k1, k2, k3, part, uall, cm, cs, idv, cpart, rpart,
    xs_s, xs_r, ys_s, ys_r, yf_s, yf_r, la_s, la_r, g_s, g_r, id_s, id_r, cy_s, cy_r, ex_s, ex_r, rr_s, rr_r, loc, in_sem, lists, counts,
):
    mrow, srow, keep = (m0, m1, m2, m3), (s0, s1, s2, s3), (k0, k1, k2, k3)
    row = lax.axis_index("row")
    col = lax.axis_index("col")
    yme, xme = col // SIDE, col % SIDE
    core = row % 2
    half = LAT // 2
    sibling = (row + 1 - 2 * core, col)

    def xpeer(i):
        return (row, yme * SIDE + (xme + OFFSETS[i]) % SIDE)

    def ypeer(i):
        return (row, ((yme + OFFSETS[i]) % SIDE) * SIDE + xme)

    def zpeer(d):
        return ((row + 2 * d) % ROWS, col)

    barrier = pltpu.get_barrier_semaphore()
    for i in range(1, SIDE):
        pl.semaphore_signal(barrier, inc=1, device_id=xpeer(i), device_id_type=MESH)
        pl.semaphore_signal(barrier, inc=1, device_id=ypeer(i), device_id_type=MESH)
    for d in range(1, ROWS // 2):
        pl.semaphore_signal(barrier, inc=1, device_id=zpeer(d), device_id_type=MESH)
    pl.semaphore_signal(barrier, inc=1, device_id=sibling, device_id_type=MESH)

    loads = [
        pltpu.make_async_copy(a, b, in_sem.at[n])
        for n, (a, b) in enumerate((
            (x_ref, xg.at[0]), (y_ref, yg.at[0]), (la_ref, lag.at[xme]), (g_ref, gg.at[0]),
            (lists_ref, lists), (counts_ref, counts)))
    ]
    for copy in loads:
        copy.start()
    rhs[SIDE * TBC] = jnp.concatenate(
        [jnp.zeros((96, BC), jnp.bfloat16)]
        + [bias_rows([None] * 3, [jnp.full((1, BC), NEG, jnp.float32)] + [jnp.zeros((1, BC), jnp.float32)] * 2)]
        + [jnp.zeros((128, BC), jnp.bfloat16)], axis=0)

    def init(xi, _):
        for b in range(SBD):
            mrow[b][xi] = jnp.full((BC, 128), NEG, jnp.float32)
            srow[b][xi] = jnp.zeros((BC, 128), jnp.float32)
        return 0

    lax.fori_loop(0, SIDE, init, 0)

    for copy in loads:
        copy.wait()
    slot = lax.broadcasted_iota(jnp.int32, (KC, ROWS * SBD), 0)
    idg[0] = jnp.full((8, 128), NOSLOT, jnp.int32)
    idg[0, :KC, :ROWS * SBD] = jnp.where(slot < counts[...], lists[...], NOSLOT)

    pl.semaphore_wait(barrier, 2 * (SIDE - 1) + ROWS // 2)

    def remote(src, dst, s, r, dev):
        return pltpu.make_async_remote_copy(
            src_ref=src, dst_ref=dst, send_sem=s, recv_sem=r, device_id=dev, device_id_type=MESH)

    mine = pl.ds(pl.multiple_of(core * half, half), half)
    theirs = pl.ds(pl.multiple_of((1 - core) * half, half), half)

    def sends(i):
        t = THERE[i]
        return [
            remote(xg.at[0], xg.at[t], xs_s.at[t], xs_r.at[t], xpeer(i)),
            remote(yg.at[0, mine], yg.at[t, mine], ys_s.at[t], ys_r.at[t], ypeer(i)),
            remote(idg.at[0], idg.at[t], id_s.at[t], id_r.at[t], ypeer(i)),
            remote(gg.at[0], gg.at[t], g_s.at[t], g_r.at[t], ypeer(i)),
            remote(lag.at[xme], lag.at[xme], la_s.at[t], la_r.at[t], xpeer(i)),
        ]

    def row_send(i, a):
        return remote(part.at[0, a], part.at[THERE[i], a], ex_s.at[i, a], ex_r.at[THERE[i], a], xpeer(i))

    def col_send(i):
        return remote(cpart.at[i], rpart.at[0, THERE[i]], cy_s.at[i], cy_r.at[THERE[i]], ypeer(i))

    def pair_send():
        return remote(cpart.at[SIDE], rpart.at[1, 0], rr_s.at[0], rr_r.at[0], sibling)

    def last_send(d):
        return remote(cpart.at[SIDE + 1], rpart.at[1, ROWS // 2 - d], rr_s.at[d], rr_r.at[ROWS // 2 - d], zpeer(d))

    for i in (1, 2):
        for copy in sends(i):
            copy.start()

    def await_x(i):
        remote(xg.at[0], xg.at[i], xs_s.at[i], xs_r.at[i], sibling).wait_recv()

    def forward_y(i):
        remote(yg.at[0, mine], yg.at[i, mine], ys_s.at[i], ys_r.at[i], sibling).wait_recv()
        remote(yg.at[i, mine], yg.at[i, mine], yf_s.at[i], yf_r.at[i], sibling).start()

    def await_y(i):
        remote(yg.at[i, mine], yg.at[i, theirs], yf_s.at[i], yf_r.at[i], sibling).wait()
        remote(gg.at[0], gg.at[i], g_s.at[i], g_r.at[i], sibling).wait_recv()
        remote(idg.at[0], idg.at[i], id_s.at[i], id_r.at[i], sibling).wait_recv()

    def prep_x(i):
        def one(b, _):
            v = xg[i, :, pl.ds(pl.multiple_of(b * BC, BC), BC)]
            hi, mid, low = split3(v * KAPPA)
            norm = jnp.sum(v * v, axis=0, keepdims=True) * (-0.5 * KAPPA)
            z = jnp.concatenate(
                [hi, mid, low, bias_rows(split3(norm), [None] * 3), hi, mid, hi, jnp.zeros((LAT, BC), jnp.bfloat16)], axis=0)
            lhs[i * SBD + b] = z.T
            return 0

        lax.fori_loop(0, SBD, one, 0)

    def prep_y(i):
        def one(t, _):
            v = yg[i, :, pl.ds(pl.multiple_of(t * BC, BC), BC)]
            hi, mid, low = split3(v)
            bias = jnp.concatenate([gg[i, pl.ds(2 * t, 1), :], gg[i, pl.ds(2 * t + 1, 1), :]], axis=1) * KAPPA - jnp.sum(v * v, axis=0, keepdims=True) * (0.5 * KAPPA)
            rhs[i * TBC + t] = jnp.concatenate(
                [hi, hi, hi, bias_rows([None] * 3, split3(bias)), mid, mid, low, jnp.zeros((LAT, BC), jnp.bfloat16)], axis=0)
            return 0

        lax.fori_loop(0, TBC, one, 0)
        copy = pltpu.make_async_copy(idg.at[i], ids.at[i], loc)
        copy.start()
        copy.wait()

    def listed(xi, yi, b, k):
        return ids[yi, k, (yme * SIDE + (xme + gray(xi)) % SIDE) * SBD + b]

    def score(xi, yi, b, k):
        t = listed(xi, yi, b, k)
        t = jnp.where(t == NOSLOT, SIDE * TBC, yi * TBC + t)
        return jnp.dot(lhs[xi * SBD + b], rhs[t], preferred_element_type=jnp.float32)

    def row_step(xi, yi, kept):
        tops, tiles = {}, {}

        def scores(b):
            top = mrow[b][xi]
            for k in range(KC):
                v = score(xi, yi, b, k)
                if kept:
                    keep[b][(yi * SIDE + xi) * KC + k] = v
                    v = keep[b].at[(yi * SIDE + xi) * KC + k]
                top = jnp.maximum(top, jnp.maximum(v[:, :128], v[:, 128:]))
                tiles[b, k] = v
            tops[b] = top

        def sums(b):
            top = tops[b]
            total = srow[b][xi] * jnp.exp2(mrow[b][xi] - top)
            for k in range(KC):
                v = tiles[b, k]
                total = total + (jnp.exp2(v[:, :128] - top) + jnp.exp2(v[:, 128:] - top))
            mrow[b][xi] = top
            srow[b][xi] = total

        for b in range(SBD):
            scores(b)
            sums(b)

    def first(s, _):
        early = s < 9
        xi = jnp.where(early, s % 3, SIDE - 1)
        yi = jnp.where(early, s // 3, s - 9)

        @pl.when((s == 1) | (s == 2) | (s == 9))
        def _():
            await_x(xi)

        @pl.when(s == 1)
        def _():
            for copy in sends(3):
                copy.start()
            forward_y(1)
            forward_y(2)

        @pl.when(s == 9)
        def _():
            forward_y(3)

        @pl.when((s == 3) | (s == 6))
        def _():
            await_y(yi)

        @pl.when((s < 3) | (s == 9))
        def _():
            prep_x(xi)

        @pl.when((s == 0) | (s == 3) | (s == 6))
        def _():
            prep_y(yi)

        row_step(xi, yi, True)
        return 0

    lax.fori_loop(0, 12, first, 0)
    await_y(3)
    prep_y(3)

    lane = lax.broadcasted_iota(jnp.int32, (BC, 128), 1)

    def second(a, _):
        xi = gray((a - xme + SIDE) % SIDE)
        row_step(xi, SIDE - 1, False)
        out = jnp.zeros((BC, 128), jnp.float32)
        for b in range(SBD):
            m = mrow[b][xi]
            top = jnp.max(m, axis=1, keepdims=True)
            total = jnp.sum(srow[b][xi] * jnp.exp2(m - top), axis=1, keepdims=True)
            out = jnp.where(lane == b, top + jnp.log2(total), out)
        part[0, a] = out.T[:8]
        for i in range(1, SIDE):
            row_send(i, a).start()
        return 0

    lax.fori_loop(0, SIDE, second, 0)
    for i in range(1, SIDE):
        remote(lag.at[xme], lag.at[0], la_s.at[i], la_r.at[i], sibling).wait_recv()

    def potential(a):
        xi = gray((a - xme + SIDE) % SIDE)
        parts = [part[0, a]]
        for i in range(1, SIDE):
            remote(part.at[0, a], part.at[i, a], ex_s.at[i, a], ex_r.at[i, a], sibling).wait_recv()
            parts.append(part[i, a])
        top = functools.reduce(jnp.maximum, parts)
        lse = top + jnp.log2(sum(jnp.exp2(v - top) for v in parts))
        mass = jnp.concatenate(
            [jnp.concatenate([lag[a, 2 * b:2 * b + 1], lag[a, 2 * b + 1:2 * b + 2]], axis=1) for b in range(SBD)]
            + [jnp.zeros((8 - SBD, BC), jnp.float32)], axis=0)
        u = mass * LOG2E - lse
        for b in range(SBD):
            for h in range(2):
                uall[a, 2 * b + h:2 * b + h + 1, :] = u[b:b + 1, h * 128:(h + 1) * 128]
        across = jnp.concatenate([u, jnp.zeros((120, BC), jnp.float32)], axis=0).T
        for b in range(SBD):
            mrow[b][xi] = jnp.broadcast_to(across[:, b:b + 1], (BC, 128))
        return xi

    def col_step(xi, yi, kept):
        for b in range(SBD):
            vs = []
            for k in range(KC):
                vs.append(keep[b].at[(yi * SIDE + xi) * KC + k] if kept else score(xi, yi, b, k))
                idv[yi * SIDE + xi, b * KC + k:b * KC + k + 1, :] = jnp.full((1, BC), listed(xi, yi, b, k), jnp.int32)
            for h in range(2):
                lanes = slice(h * 128, (h + 1) * 128)
                ps = [[] for _ in range(KC)]
                ts = [[] for _ in range(KC)]
                for r in range(0, BC, 64):
                    rows = slice(r, r + 64)
                    u = mrow[b][xi, rows]
                    for k in range(KC):
                        t = (vs[k][rows, lanes] + u).reshape(64 // 8, 8, 128)
                        p = jnp.max(t, axis=0)
                        ps[k].append(p)
                        ts[k].append(jnp.sum(jnp.exp2(t - p), axis=0))
                for k in range(KC):
                    at = b * KC + k
                    m8 = functools.reduce(jnp.maximum, ps[k])
                    peak = jnp.max(m8, axis=0, keepdims=True)
                    total = sum(q * jnp.exp2(p - peak) for q, p in zip(ts[k], ps[k]))
                    cm[yi * SIDE + xi, at:at + 1, lanes] = peak
                    cs[yi * SIDE + xi, at:at + 1, lanes] = jnp.sum(total, axis=0, keepdims=True)

    def finish_cols(yi):
        group = pl.ds(yi * SIDE, SIDE)
        ids_v = idv[group].reshape(-1, BC)
        m = cm[group].reshape(-1, BC)
        c = cs[group].reshape(-1, BC)
        peaks, totals = [], []
        for t in range(TBC):
            hit = ids_v == t
            peak = jnp.max(jnp.where(hit, m, NEG), axis=0, keepdims=True)
            peaks.append(peak)
            totals.append(jnp.sum(jnp.where(hit, c * jnp.exp2(m - peak), 0.0), axis=0, keepdims=True))
        peak = jnp.concatenate(peaks, axis=0)
        total = jnp.concatenate(totals, axis=0)
        some = total > 0.0
        value = jnp.where(some, peak + jnp.log2(jnp.where(some, total, 1.0)), NEG)
        for t in range(TBC):
            for h in range(2):
                cpart[yi, 2 * t + h:2 * t + h + 1, :] = value[t:t + 1, h * 128:(h + 1) * 128]

    def third(a, _):
        col_step(potential(a), SIDE - 1, False)
        return 0

    lax.fori_loop(0, SIDE, third, 0)
    f_ref[...] = uall[xme]
    finish_cols(SIDE - 1)
    col_send(3).start()

    def fourth(yi):
        def body(xi, _):
            col_step(xi, yi, True)
            return 0

        lax.fori_loop(0, SIDE, body, 0)
        finish_cols(yi)

    def fourth_pair(q, _):
        fourth(q)
        return 0

    lax.fori_loop(1, 3, fourth_pair, 0)
    for i in (1, 2):
        col_send(i).start()
    fourth(0)

    def join(values):
        peak = functools.reduce(jnp.maximum, values)
        return peak + jnp.log2(sum(jnp.exp2(v - peak) for v in values))

    values = [cpart[0]]
    for i in range(1, SIDE):
        remote(cpart.at[0], rpart.at[0, i], cy_s.at[i], cy_r.at[i], sibling).wait_recv()
        values.append(rpart[0, i])
    cpart[SIDE] = join(values)
    pair_send().start()
    remote(cpart.at[SIDE], rpart.at[1, 0], rr_s.at[0], rr_r.at[0], sibling).wait_recv()
    both = join([cpart[SIDE], rpart[1, 0]])
    cpart[SIDE + 1] = both
    for d in range(1, ROWS // 2):
        last_send(d).start()
    values = [both]
    for d in range(1, ROWS // 2):
        remote(cpart.at[SIDE], rpart.at[1, d], rr_s.at[d], rr_r.at[d], sibling).wait_recv()
        values.append(rpart[1, d])
    gp_ref[...] = join(values)
    for i in range(1, SIDE):
        for copy in sends(i) + [col_send(i)] + [row_send(i, a) for a in range(SIDE)]:
            copy.wait_send()
    pair_send().wait_send()
    for d in range(1, ROWS // 2):
        last_send(d).wait_send()


def finish(u_ref, lse_ref, g_ref, lb_ref, f_ref, gp_ref):
    f_ref[...] = u_ref[...] * (EPSILON * LN2)
    gp_ref[...] = EPSILON * lb_ref[...] - (EPSILON * LN2) * (lse_ref[...] - g_ref[...] * KAPPA)


def per_device(src_emb, tgt_emb, log_a, log_b, g_init, lists, counts):
    f32, bf16 = jnp.float32, jnp.bfloat16
    dma4 = pltpu.SemaphoreType.DMA((SIDE,))
    u, lse = pl.pallas_call(
        kernel,
        out_shape=(jax.ShapeDtypeStruct((8, 128), f32), jax.ShapeDtypeStruct((16, 128), f32)),
        in_specs=[pl.BlockSpec(memory_space=pl.ANY)] * 6,
        out_specs=(pl.BlockSpec(memory_space=pltpu.VMEM),) * 2,
        scratch_shapes=[
            pltpu.VMEM((SIDE, LAT, SBD * BC), f32),
            pltpu.VMEM((SIDE, LAT, TBC * BC), f32),
            pltpu.VMEM((SIDE, 8, 128), f32),
            pltpu.VMEM((SIDE, 16, 128), f32),
            pltpu.VMEM((SIDE, 8, 128), jnp.int32),
            pltpu.SMEM((SIDE, 8, 128), jnp.int32),
            pltpu.VMEM((SIDE * SBD, BC, 256), bf16),
            pltpu.VMEM((SIDE * TBC + 1, 256, BC), bf16),
        ] + [pltpu.VMEM((SIDE, BC, 128), f32)] * (2 * SBD) + [pltpu.VMEM((STORED, BC, BC), f32)] * SBD + [
            pltpu.VMEM((SIDE, SIDE, 8, BC), f32),
            pltpu.VMEM((SIDE, 8, 128), f32),
            pltpu.VMEM((SIDE * SIDE, SBD * KC, BC), f32),
            pltpu.VMEM((SIDE * SIDE, SBD * KC, BC), f32),
            pltpu.VMEM((SIDE * SIDE, SBD * KC, BC), jnp.int32),
            pltpu.VMEM((SIDE + 2, 16, 128), f32),
            pltpu.VMEM((2, ROWS, 16, 128), f32),
        ] + [dma4] * 14 + [pltpu.SemaphoreType.DMA((SIDE, SIDE))] * 2 + [pltpu.SemaphoreType.DMA((ROWS // 2,))] * 2 + [
            pltpu.SemaphoreType.DMA,
            pltpu.SemaphoreType.DMA((6,)),
            pltpu.VMEM((KC, ROWS * SBD), jnp.int32),
            pltpu.VMEM((1, ROWS * SBD), jnp.int32),
        ],
        compiler_params=pltpu.CompilerParams(
            collective_id=0, has_side_effects=True, vmem_limit_bytes=63 * 2**20),
        name="sinkhorn",
    )(src_emb, tgt_emb, log_a.reshape(8, 128), g_init.reshape(16, 128),
      lists.transpose(1, 2, 0).reshape(KC, ROWS * SBD), counts.reshape(1, ROWS * SBD))
    f, g = pl.pallas_call(
        finish,
        out_shape=(jax.ShapeDtypeStruct((8, 128), f32), jax.ShapeDtypeStruct((16, 128), f32)),
        in_specs=[pl.BlockSpec(memory_space=pltpu.VMEM)] * 4,
        out_specs=(pl.BlockSpec(memory_space=pltpu.VMEM),) * 2,
        name="finish",
    )(u, lse, g_init.reshape(16, 128), log_b.reshape(16, 128))
    return f.reshape(-1), g.reshape(-1)


def solution(mesh):
    in_specs = (
        P(None, ("row", "col")),
        P(None, "col"),
        P(("row", "col")),
        P("col"),
        P("col"),
        P("row", "col", None),
        P("row", "col"),
    )
    return jax.shard_map(
        per_device, mesh=mesh, in_specs=in_specs, out_specs=(P(("row", "col")), P("col")), check_vma=False)
```
